512 devices in a mesh: irrep: 8 (over y, core), tile: 64 (over z, x).
Axes of the slice: x: 4, y: 4, z: 16, core: 2. Of those that a mesh axis runs over, the one named last changes fastest.
Arguments:
- amplitudes: bfloat16 [8, 1024, 64, 256], P('irrep', 'tile'), may hold values from -6 to 6
- integrals: bfloat16 [8, 64, 256, 256], P('irrep', 'tile'), may hold values from -0.375 to 0.375
- executors: int32 [8, 1024, 2], P('irrep', 'tile'), may hold values from 0 to 63, all different within a row; in each aligned block of 16 rows (0 to 15, 16 to 31, ..., all dimensions but the last counted through in order) at most 2 rows name the same one
- residual_slots: int32 [8, 1024, 2], P('irrep', 'tile'), may hold values from 0 to 7
Outputs:
- residual: bfloat16 [8, 512, 64, 256], P('irrep', 'tile')
The draws below stay inside these ranges and needn't reach their ends.
Inputs may be any that keep to these rules, and one draw needn't show every extreme that they name: `executors`: within a row the 2 entries differ. Within the 16 rows of one device no value appears more than 2 times.
All inputs are finite; a program needn't handle non-finite values.
Results may differ from the reference program's by a relative error of at most 0.005.
Values may be sent and summed in bfloat16 or wider, within the bound.
No kernel may reach another device: no remote copies, remote signals or barrier semaphores. Data moves between devices by JAX's collectives and lax.ppermute only.
A program may use at most 64 MiB of HBM per device.

```python
import math
import jax
import jax.numpy as jnp
import numpy as np
from jax import lax

TILE = 256
ROWS = 64
AT = 16
TOP = 2
RT = 8
CAP = 2
N_IRREP = 8
N_TILE = 64


def plant(values, key, least, top_value):
    dims = values.shape
    index_at = [jax.random.randint(jax.random.fold_in(key, axis), (), 0, dims[axis]) for axis in range(len(dims))]
    values = values.at[tuple(index_at)].set(least)
    longest = dims.index(max(dims))
    index_at[longest] = (index_at[longest] + 1) % dims[longest]
    return values.at[tuple(index_at)].set(top_value)


def levels(rng, dims, cuts, least, high):
    loudness = 1.0
    for dim, parts in cuts:
        steps = jax.random.uniform(jax.random.fold_in(jax.random.fold_in(rng, 6), dim), (parts,), jnp.float32, least / len(cuts), high / len(cuts))
        loudness = loudness * jnp.repeat(jnp.exp(steps), dims[dim] // parts).reshape((-1,) + (1,) * (len(dims) - 1 - dim))
    return loudness


def assign_block(rng, own, number, rows, amount, top, reach, skew):
    sequence = jax.random.permutation(rng, amount)
    heavy_load, ordinary = load_shares(amount, rows * top, reach, skew, True), load_shares(amount, rows * top, reach, skew, False)
    places = jnp.arange(amount)

    def named(lengths, turn):
        used = int((lengths > 0).sum())
        fixed = max(1, used // 4)
        moved = fixed + (places - fixed + turn * (used - fixed)) % max(1, amount - fixed)
        return jnp.zeros((amount,), jnp.int32).at[sequence[jnp.where(places < fixed, places, moved)]].set(jnp.asarray(lengths, jnp.int32))

    lengths = jnp.where(number % 4 == 0, named(heavy_load, number // 4), named(ordinary, number - number // 4 - 1))
    mixed = jax.random.permutation(jax.random.fold_in(own, 3), amount)
    giver, sink = mixed[0:amount // 2 * 2:2], mixed[1:amount // 2 * 2:2]
    margin = jnp.minimum(lengths[giver] - 1, reach - lengths[sink]) // 2
    margin = jnp.where((giver == sequence[0]) | (sink == sequence[0]) | (lengths[sink] == 0), 0, jnp.maximum(margin, 0))
    moved = jax.random.randint(jax.random.fold_in(own, 4), (amount // 2,), 0, 1 << 20) % (margin + 1)
    lengths = lengths.at[giver].add(-moved).at[sink].add(moved)
    labels = jnp.searchsorted(jnp.cumsum(lengths), jnp.arange(rows * top), side="right").astype(jnp.int32)
    grid = labels.reshape(top, rows).T
    grid = grid[jax.random.permutation(jax.random.fold_in(own, 1), rows)]
    turn = jax.random.randint(jax.random.fold_in(own, 2), (rows, 1), 0, top)
    return jnp.take_along_axis(grid, (jnp.arange(top)[None, :] + turn) % top, axis=1)


def load_shares(number_of, total, reach, slope, full):
    weights = [(1 << 20) // math.isqrt(grade ** slope) + 1 for grade in range(1, number_of + 1)]
    largest = reach if full else min(reach, max(-(-total // number_of), total * weights[0] // sum(weights)))
    least = 1 if total - largest >= number_of - 1 else 0
    given, rest = [largest] + [least] * (number_of - 1), total - largest - least * (number_of - 1)
    while rest > 0:
        movable = [i for i in range(1, number_of) if given[i] < largest] or [i for i in range(1, number_of) if given[i] < reach]
        whole, remaining = sum([weights[i] for i in movable]), rest
        for i in movable:
            addition = min(reach - given[i], max(1, remaining * weights[i] // whole), rest)
            given[i] = given[i] + addition
            rest = rest - addition
    return np.array(given)


def centred(rng, dims, deviation, most, shards=(), kind=jnp.bfloat16):
    array = jax.random.normal(rng, dims, jnp.float32) * deviation
    if len(shards) > 0:
        array = levels(rng, dims, shards, -0.22, 0.18) * array
    return jnp.clip(array, min=-most, max=most).astype(kind)


def setup_inputs(seed: int = 0) -> dict:
    seeds = jax.random.split(jax.random.key(seed), 5)
    amplitudes = centred(seeds[0], (N_IRREP, N_TILE * AT, ROWS, TILE), 1.0, 6.0, ((0, 8), (1, 64)))
    integrals = centred(seeds[1], (N_IRREP, N_TILE, TILE, TILE), TILE ** -0.5, 0.375, ((0, 8), (1, 64)))
    executors_keys = jax.random.split(jax.random.fold_in(seeds[2], 1), N_IRREP * (N_TILE * AT) // AT)
    executors_turns = jax.random.permutation(jax.random.fold_in(seeds[2], 3), N_IRREP * (N_TILE * AT) // AT)
    executors = jax.vmap(lambda own, number: assign_block(jax.random.fold_in(seeds[2], 2), own, number, AT, N_TILE, TOP, CAP, 2))(executors_keys, executors_turns).reshape((N_IRREP, N_TILE * AT, TOP))
    residual_slots = plant(jax.random.randint(seeds[3], (N_IRREP, N_TILE * AT, TOP), 0, RT), jax.random.fold_in(seeds[3], 1), 0, RT - 1).astype(jnp.int32)
    return dict(amplitudes=amplitudes, integrals=integrals, executors=executors, residual_slots=residual_slots)


def reference(amplitudes, integrals, executors, residual_slots):
    device_count = N_IRREP * N_TILE
    own_all = amplitudes.reshape(device_count, AT, ROWS, TILE)
    target_all = executors.reshape(device_count, AT, TOP)
    slot_all = residual_slots.reshape(device_count, AT, TOP)
    partner_all = jnp.bitwise_xor(jnp.arange(device_count, dtype=jnp.int32) // N_TILE, 1).astype(jnp.int32)

    def one_device(inputs):
        own_tiles, targets, slots, partner = inputs
        block_tiles = lax.dynamic_index_in_dim(integrals, partner, 0, keepdims=False)
        selected = jnp.take(block_tiles, targets, axis=0).astype(jnp.float32)
        products = jnp.einsum("arw,akwv->akrv", own_tiles.astype(jnp.float32), selected, precision=lax.Precision.HIGHEST)
        rounded = lax.optimization_barrier(products.astype(jnp.bfloat16)).astype(jnp.float32)
        onehot = (slots[..., None] == jnp.arange(RT, dtype=jnp.int32)).astype(jnp.float32)
        summed = jnp.einsum("akn,akrv->nrv", onehot, rounded, precision=lax.Precision.HIGHEST)
        return summed.astype(jnp.bfloat16)

    result = lax.map(one_device, (own_all, target_all, slot_all, partner_all))
    return result.reshape(N_IRREP, N_TILE * RT, ROWS, TILE)
```

```python
import functools
import jax
import jax.numpy as jnp
from jax import lax
from jax.experimental import pallas as pl
from jax.experimental.pallas import tpu as pltpu
from jax.sharding import PartitionSpec as P

RT = 8
XS = 4
META = 16

OFFSETS = (0, -5, 5, -1, -6, 4, 1, -4, 6, -2, -7, 3, 2, -3, 7, -8)


def moved(block, dz, flip=False):
    groups, tiles = lax.axis_size("irrep"), lax.axis_size("tile")
    route = []
    for g in range(groups):
        for t in range(tiles):
            to = (g ^ 1 if flip else g) * tiles + (t + dz * XS) % tiles
            route.append((g * tiles + t, to))
    return lax.ppermute(block, ("irrep", "tile"), route)


def along_x(block):
    tiles = lax.axis_size("tile")
    rows = [list(range(low, low + XS)) for low in range(0, tiles, XS)]
    return lax.all_to_all(
        block, "tile", split_axis=0, concat_axis=0, axis_index_groups=rows, tiled=True
    )


def ladder(listed, counts, amps, *refs):
    held, out, total = refs[:-2], refs[-2], refs[-1]
    rows = total.shape[1]
    own = (amps.shape[1] - META) // rows
    total[...] = jnp.zeros_like(total)
    place = 0
    for ref in held:
        for k in range(ref.shape[0]):

            def pair(q, carry, ref=ref, k=k, place=place):
                codes = [listed[place * 8 + 2 * q + i] for i in range(2)]
                tiles = []
                for code in codes:
                    tile = code >> 6
                    start = pl.multiple_of((tile % own) * rows, rows)
                    tiles.append(amps[tile // own, pl.ds(start, rows), :])
                product = jnp.dot(
                    jnp.concatenate(tiles, axis=0), ref[k], preferred_element_type=jnp.float32
                )
                for i, code in enumerate(codes):
                    total[code & 63] += product[i * rows : (i + 1) * rows]
                return carry

            pair(0, 0)
            lax.fori_loop(1, (counts[place] + 1) // 2, pair, 0)
            place += 1
    out[...] = total[: out.shape[0]].astype(out.dtype)


def per_device(amplitudes, integrals, executors, residual_slots):
    own, rows, columns = amplitudes.shape[1:]
    fanout = executors.shape[2]
    tasks = own * fanout
    depth = lax.axis_size("tile") // XS
    me = lax.axis_index("tile")
    my_x, my_z = me % XS, me // XS

    first = integrals[0]
    near = jnp.concatenate([moved(first, dz, True) for dz in (0, 5, -5)], axis=0)
    up, down = moved(near, 1), moved(near, -1)
    upper, lower = moved(up, 1), moved(down, -1)
    last = moved(up[1:2], 2)

    numbers = jnp.concatenate([executors.reshape(tasks), residual_slots.reshape(tasks)])
    meta = jnp.pad(numbers.astype(jnp.bfloat16)[None, :], ((0, META - 1), (0, columns - 2 * tasks)))
    packed = jnp.concatenate([amplitudes.reshape(own * rows, columns), meta], axis=0)
    amps = along_x(jnp.broadcast_to(packed, (XS,) + packed.shape))

    numbers = amps[:, own * rows, : 2 * tasks].astype(jnp.int32)
    target = numbers[:, :tasks].reshape(XS * tasks)
    slot = numbers[:, tasks:].reshape(XS * tasks)
    task = jnp.arange(XS * tasks, dtype=jnp.int32)
    code = (task // fanout) * 64 + (task // tasks) * RT + slot
    apart = (target // XS - my_z) % depth
    offsets = jnp.array([o % depth for o in OFFSETS], jnp.int32)
    hot = (apart[None, :] == offsets[:, None]) & (target % XS == my_x)[None, :]
    hot_bf16 = hot.astype(jnp.bfloat16)
    earlier = (task[:, None] < task[None, :]).astype(jnp.bfloat16)
    rank = jnp.dot(hot_bf16, earlier, preferred_element_type=jnp.float32).astype(jnp.int32)
    counts = jnp.sum(hot.astype(jnp.int32), axis=1)
    ranks = jnp.arange(8, dtype=jnp.int32)
    chosen = hot[:, None, :] & (rank[:, None, :] == ranks[None, :, None])
    spare = XS * RT
    listed = spare + jnp.sum(jnp.where(chosen, code - spare, 0), axis=2)

    vmem = pl.BlockSpec(memory_space=pltpu.VMEM)
    smem = pl.BlockSpec(memory_space=pltpu.SMEM)
    held = (near, up, down, upper, lower, last)
    partial = pl.pallas_call(
        ladder,
        out_shape=jax.ShapeDtypeStruct((XS * RT, rows, columns), jnp.bfloat16),
        in_specs=[smem, smem, vmem] + [vmem] * len(held),
        out_specs=vmem,
        scratch_shapes=[pltpu.VMEM((XS * RT + 1, rows, columns), jnp.float32)],
        compiler_params=pltpu.CompilerParams(vmem_limit_bytes=24 * 1024 * 1024),
        cost_estimate=pl.CostEstimate(
            flops=2 * tasks * rows * columns * columns, bytes_accessed=1 << 23, transcendentals=0
        ),
    )(listed.reshape(depth * 8), counts, amps, *held)
    back = along_x(partial).reshape(XS, RT, rows, columns)
    return jnp.sum(back.astype(jnp.float32), axis=0).astype(jnp.bfloat16)[None]


def solution(mesh):
    placed = (
        P("irrep", "tile", None, None),
        P("irrep", "tile", None, None),
        P("irrep", "tile", None),
        P("irrep", "tile", None),
    )
    return jax.shard_map(
        per_device,
        mesh=mesh,
        in_specs=placed,
        out_specs=P("irrep", "tile", None, None),
        check_vma=False,
    )
```

```python
import functools
import jax
import jax.numpy as jnp
from jax import lax
from jax.experimental import pallas as pl
from jax.experimental.pallas import tpu as pltpu
from jax.sharding import PartitionSpec as P

RT = 8
XS = 4
SKIP = 4

META = 16

APART = (0,) * 4 + (-1,) * 4 + (1,) * 4 + (2,) * 4


def moved(block, dz, flip=False):
    groups, tiles = lax.axis_size("irrep"), lax.axis_size("tile")
    route = []
    for g in range(groups):
        for t in range(tiles):
            to = (g ^ 1 if flip else g) * tiles + (t + dz * XS) % tiles
            route.append((g * tiles + t, to))
    return lax.ppermute(block, ("irrep", "tile"), route)


def along_x(block):
    tiles = lax.axis_size("tile")
    rows = [list(range(low, low + XS)) for low in range(0, tiles, XS)]
    return lax.all_to_all(
        block, "tile", split_axis=0, concat_axis=0, axis_index_groups=rows, tiled=True
    )


def every_fourth(block):
    tiles = lax.axis_size("tile")
    step = SKIP * XS
    groups = [list(range(low, tiles, step)) for low in range(step)]
    return lax.all_gather(block, "tile", axis=0, axis_index_groups=groups, tiled=True)


def pack(amps, targets, slots, out, meta, sems):
    size, (fanout, count) = amps.shape[0], targets.shape
    copies = [
        pltpu.make_async_copy(amps, out.at[x, pl.ds(0, size)], sems.at[x]) for x in range(XS)
    ]
    for copy in copies:
        copy.start()
    numbers = jnp.concatenate([targets[...], slots[...]], axis=0).astype(jnp.float32)
    numbers = jnp.pad(numbers, ((0, meta.shape[0] - 2 * fanout), (0, meta.shape[1] - count)))
    meta[...] = numbers.astype(meta.dtype)
    for x in range(XS):
        copies.append(
            pltpu.make_async_copy(
                meta, out.at[x, pl.ds(size, meta.shape[0])], sems.at[XS + x]
            )
        )
        copies[-1].start()
    for copy in copies:
        copy.wait()


def ladder(first, listed, counts, amps, *refs):
    held, out, total = refs[:-2], refs[-2], refs[-1]
    rows = total.shape[1]
    own = (amps.shape[1] - META) // rows
    if first:
        total[...] = held[0][...]
        held = held[1:]
    else:
        total[...] = jnp.zeros_like(total)
    place = first
    for ref in held:
        for k in range(ref.shape[0]):

            def pair(q, carry, ref=ref, k=k, place=place):
                codes = [listed[place * 8 + 2 * q + i] for i in range(2)]
                tiles = []
                for code in codes:
                    tile = code >> 6
                    start = pl.multiple_of((tile % own) * rows, rows)
                    tiles.append(amps[tile // own, pl.ds(start, rows), :])
                product = jnp.dot(
                    jnp.concatenate(tiles, axis=0), ref[k], preferred_element_type=jnp.float32
                )
                for i, code in enumerate(codes):
                    total[code & 63] += product[i * rows : (i + 1) * rows]
                return carry

            pair(0, 0)
            lax.fori_loop(1, (counts[place] + 1) // 2, pair, 0)
            place += 1
    out[...] = total[: out.shape[0]].astype(out.dtype)


def multiply(first, listed, counts, amps, held, out_shape, out_dtype):
    vmem = pl.BlockSpec(memory_space=pltpu.VMEM)
    smem = pl.BlockSpec(memory_space=pltpu.SMEM)
    rows, columns = held[-1].shape[-2] // 4, held[-1].shape[-1]
    spare_shape = (XS * RT + 1, rows, columns)
    return pl.pallas_call(
        functools.partial(ladder, first),
        out_shape=jax.ShapeDtypeStruct(out_shape, out_dtype),
        in_specs=[smem, smem, vmem] + [vmem] * len(held),
        out_specs=vmem,
        scratch_shapes=[pltpu.VMEM(spare_shape, jnp.float32)],
        compiler_params=pltpu.CompilerParams(vmem_limit_bytes=24 * 1024 * 1024),
        cost_estimate=pl.CostEstimate(
            flops=1 << 28, bytes_accessed=1 << 23, transcendentals=0
        ),
    )(listed, counts, amps, *held)


def per_device(amplitudes, integrals, executors, residual_slots):
    own, rows, columns = amplitudes.shape[1:]
    fanout = executors.shape[2]
    tasks = own * fanout
    depth = lax.axis_size("tile") // XS
    me = lax.axis_index("tile")
    my_x, my_z = me % XS, me // XS

    vmem = pl.BlockSpec(memory_space=pltpu.VMEM)
    anywhere = pl.BlockSpec(memory_space=pl.ANY)
    flat = own * rows
    packed = pl.pallas_call(
        pack,
        out_shape=jax.ShapeDtypeStruct((XS, flat + META, columns), jnp.bfloat16),
        in_specs=[vmem, vmem, vmem],
        out_specs=anywhere,
        scratch_shapes=[
            pltpu.VMEM((META, columns), jnp.bfloat16),
            pltpu.SemaphoreType.DMA((2 * XS,)),
        ],
    )(amplitudes.reshape(flat, columns), executors[0].T, residual_slots[0].T)
    integrals, packed = lax.optimization_barrier((integrals, packed))
    amps = along_x(packed)
    mine = every_fourth(integrals[0])
    mine, amps = lax.optimization_barrier((mine, amps))
    near, up, down = moved(mine, 0, True), moved(mine, 1, True), moved(mine, -1, True)
    upper, lower = moved(up[:2], 1), moved(down[2:], -1)

    numbers = amps[:, flat : flat + 2 * fanout, :own].astype(jnp.int32)
    target = numbers[:, :fanout].reshape(XS * tasks)
    slot = numbers[:, fanout:].reshape(XS * tasks)
    task = jnp.arange(XS * tasks, dtype=jnp.int32)
    source = task // tasks
    code = (source * own + task % own) * 64 + source * RT + slot
    place = jnp.arange(depth, dtype=jnp.int32)
    place_z = (my_z + jnp.array(APART, jnp.int32)) % SKIP + SKIP * (place % SKIP)
    hot = target[None, :] == (place_z * XS + my_x)[:, None]
    hot_bf16 = hot.astype(jnp.bfloat16)
    earlier = (task[:, None] < task[None, :]).astype(jnp.bfloat16)
    rank = jnp.dot(hot_bf16, earlier, preferred_element_type=jnp.float32).astype(jnp.int32)
    counts = jnp.sum(hot.astype(jnp.int32), axis=1)
    ranks = jnp.arange(8, dtype=jnp.int32)
    chosen = hot[:, None, :] & (rank[:, None, :] == ranks[None, :, None])
    spare = XS * RT
    listed = spare + jnp.sum(jnp.where(chosen, code - spare, 0), axis=2)
    listed = listed.reshape(depth * 8)

    total = multiply(
        0, listed, counts, amps, (near, up, down), (spare + 1, rows, columns), jnp.float32
    )
    partial = multiply(
        12, listed, counts, amps, (total, upper, lower), (spare, rows, columns), jnp.bfloat16
    )
    back = along_x(partial).reshape(XS, RT, rows, columns)
    return jnp.sum(back.astype(jnp.float32), axis=0).astype(jnp.bfloat16)[None]


def solution(mesh):
    placed = (
        P("irrep", "tile", None, None),
        P("irrep", "tile", None, None),
        P("irrep", "tile", None),
        P("irrep", "tile", None),
    )
    return jax.shard_map(
        per_device,
        mesh=mesh,
        in_specs=placed,
        out_specs=P("irrep", "tile", None, None),
        check_vma=False,
    )
```

```python
import functools
import jax
import jax.numpy as jnp
from jax import lax
from jax.experimental import pallas as pl
from jax.experimental.pallas import tpu as pltpu
from jax.sharding import PartitionSpec as P

RT = 8
XS = 4
SKIP = 4

META = 16

APART = (0,) * 4 + (1,) * 4 + (-1,) * 4 + (2,) * 4


def moved(block, dz, flip=False):
    groups, tiles = lax.axis_size("irrep"), lax.axis_size("tile")
    route = []
    for g in range(groups):
        for t in range(tiles):
            to = (t + (-dz if g % 2 else dz) * XS) % tiles
            route.append((g * tiles + t, (g ^ 1 if flip else g) * tiles + to))
    return lax.ppermute(block, ("irrep", "tile"), route)


def along_x(block):
    tiles = lax.axis_size("tile")
    rows = [list(range(low, low + XS)) for low in range(0, tiles, XS)]
    return lax.all_to_all(
        block, "tile", split_axis=0, concat_axis=0, axis_index_groups=rows, tiled=True
    )


def every_fourth(block):
    tiles = lax.axis_size("tile")
    step = SKIP * XS
    groups = [list(range(low, tiles, step)) for low in range(step)]
    return lax.all_gather(block, "tile", axis=0, axis_index_groups=groups, tiled=True)


def pack(amps, targets, slots, out, meta, sems):
    size, (fanout, count) = amps.shape[0], targets.shape
    copies = [
        pltpu.make_async_copy(amps, out.at[x, pl.ds(0, size)], sems.at[x]) for x in range(XS)
    ]
    for copy in copies:
        copy.start()
    numbers = jnp.concatenate([targets[...], slots[...]], axis=0).astype(jnp.float32)
    numbers = jnp.pad(numbers, ((0, meta.shape[0] - 2 * fanout), (0, meta.shape[1] - count)))
    meta[...] = numbers.astype(meta.dtype)
    for x in range(XS):
        copies.append(
            pltpu.make_async_copy(
                meta, out.at[x, pl.ds(size, meta.shape[0])], sems.at[XS + x]
            )
        )
        copies[-1].start()
    for copy in copies:
        copy.wait()


def ladder(first, listed, counts, amps, *refs):
    held, out, total = refs[:-2], refs[-2], refs[-1]
    rows = total.shape[1]
    own = (amps.shape[1] - META) // rows
    if first:
        total[...] = held[0][...]
        held = held[1:]
    else:
        total[...] = jnp.zeros_like(total)
    place = first
    for ref in held:
        for k in range(ref.shape[0]):

            def pair(q, carry, ref=ref, k=k, place=place):
                codes = [listed[place * 8 + 2 * q + i] for i in range(2)]
                tiles = []
                for code in codes:
                    tile = code >> 6
                    start = pl.multiple_of((tile % own) * rows, rows)
                    tiles.append(amps[tile // own, pl.ds(start, rows), :])
                product = jnp.dot(
                    jnp.concatenate(tiles, axis=0), ref[k], preferred_element_type=jnp.float32
                )
                for i, code in enumerate(codes):
                    total[code & 63] += product[i * rows : (i + 1) * rows]
                return carry

            pair(0, 0)
            lax.fori_loop(1, (counts[place] + 1) // 2, pair, 0)
            place += 1
    out[...] = total[: out.shape[0]].astype(out.dtype)


def multiply(first, listed, counts, amps, held, out_shape, out_dtype):
    vmem = pl.BlockSpec(memory_space=pltpu.VMEM)
    smem = pl.BlockSpec(memory_space=pltpu.SMEM)
    rows, columns = held[-1].shape[-2] // 4, held[-1].shape[-1]
    spare_shape = (XS * RT + 1, rows, columns)
    return pl.pallas_call(
        functools.partial(ladder, first),
        out_shape=jax.ShapeDtypeStruct(out_shape, out_dtype),
        in_specs=[smem, smem, vmem] + [vmem] * len(held),
        out_specs=vmem,
        scratch_shapes=[pltpu.VMEM(spare_shape, jnp.float32)],
        compiler_params=pltpu.CompilerParams(vmem_limit_bytes=24 * 1024 * 1024),
        cost_estimate=pl.CostEstimate(
            flops=1 << 28, bytes_accessed=1 << 23, transcendentals=0
        ),
    )(listed, counts, amps, *held)


def per_device(amplitudes, integrals, executors, residual_slots):
    own, rows, columns = amplitudes.shape[1:]
    fanout = executors.shape[2]
    tasks = own * fanout
    depth = lax.axis_size("tile") // XS
    me = lax.axis_index("tile")
    my_x, my_z = me % XS, me // XS

    vmem = pl.BlockSpec(memory_space=pltpu.VMEM)
    anywhere = pl.BlockSpec(memory_space=pl.ANY)
    flat = own * rows
    packed = pl.pallas_call(
        pack,
        out_shape=jax.ShapeDtypeStruct((XS, flat + META, columns), jnp.bfloat16),
        in_specs=[vmem, vmem, vmem],
        out_specs=anywhere,
        scratch_shapes=[
            pltpu.VMEM((META, columns), jnp.bfloat16),
            pltpu.SemaphoreType.DMA((2 * XS,)),
        ],
    )(amplitudes.reshape(flat, columns), executors[0].T, residual_slots[0].T)
    integrals, packed = lax.optimization_barrier((integrals, packed))
    amps = along_x(packed)
    mine = every_fourth(integrals[0])
    mine, amps = lax.optimization_barrier((mine, amps))
    one, near, other = moved(mine, 1, True), moved(mine, 0, True), moved(mine, -1, True)
    far = moved(one, -1)

    numbers = amps[:, flat : flat + 2 * fanout, :own].astype(jnp.int32)
    target = numbers[:, :fanout].reshape(XS * tasks)
    slot = numbers[:, fanout:].reshape(XS * tasks)
    task = jnp.arange(XS * tasks, dtype=jnp.int32)
    source = task // tasks
    code = (source * own + task % own) * 64 + source * RT + slot
    place = jnp.arange(depth, dtype=jnp.int32)
    toward = 1 - 2 * (lax.axis_index("irrep") % 2)
    apart = toward * jnp.array(APART, jnp.int32)
    place_z = (my_z + apart) % SKIP + SKIP * (place % SKIP)
    hot = target[None, :] == (place_z * XS + my_x)[:, None]
    hot_bf16 = hot.astype(jnp.bfloat16)
    earlier = (task[:, None] < task[None, :]).astype(jnp.bfloat16)
    rank = jnp.dot(hot_bf16, earlier, preferred_element_type=jnp.float32).astype(jnp.int32)
    counts = jnp.sum(hot.astype(jnp.int32), axis=1)
    ranks = jnp.arange(8, dtype=jnp.int32)
    chosen = hot[:, None, :] & (rank[:, None, :] == ranks[None, :, None])
    spare = XS * RT
    listed = spare + jnp.sum(jnp.where(chosen, code - spare, 0), axis=2)
    listed = listed.reshape(depth * 8)

    total = multiply(
        0, listed, counts, amps, (near, one, other), (spare + 1, rows, columns), jnp.float32
    )
    partial = multiply(
        12, listed, counts, amps, (total, far), (spare, rows, columns), jnp.bfloat16
    )
    back = along_x(partial).reshape(XS, RT, rows, columns)
    return jnp.sum(back.astype(jnp.float32), axis=0).astype(jnp.bfloat16)[None]


def solution(mesh):
    placed = (
        P("irrep", "tile", None, None),
        P("irrep", "tile", None, None),
        P("irrep", "tile", None),
        P("irrep", "tile", None),
    )
    return jax.shard_map(
        per_device,
        mesh=mesh,
        in_specs=placed,
        out_specs=P("irrep", "tile", None, None),
        check_vma=False,
    )
```

```python
import functools
import jax
import jax.numpy as jnp
from jax import lax
from jax.experimental import pallas as pl
from jax.experimental.pallas import tpu as pltpu
from jax.sharding import PartitionSpec as P

RT = 8
XS = 4
SKIP = 4

META = 16

APART = (0,) * 4 + (1,) * 4 + (-1,) * 4 + (2,) * 4


def moved(block, dz, flip=False):
    groups, tiles = lax.axis_size("irrep"), lax.axis_size("tile")
    route = []
    for g in range(groups):
        for t in range(tiles):
            to = (t + (-dz if g % 2 else dz) * XS) % tiles
            route.append((g * tiles + t, (g ^ 1 if flip else g) * tiles + to))
    return lax.ppermute(block, ("irrep", "tile"), route)


def along_x(block):
    tiles = lax.axis_size("tile")
    rows = [list(range(low, low + XS)) for low in range(0, tiles, XS)]
    return lax.all_to_all(
        block, "tile", split_axis=0, concat_axis=0, axis_index_groups=rows, tiled=True
    )


def every_fourth(block):
    tiles = lax.axis_size("tile")
    step = SKIP * XS
    groups = [list(range(low, tiles, step)) for low in range(step)]
    return lax.all_gather(block, "tile", axis=0, axis_index_groups=groups, tiled=True)


def pack(amps, targets, slots, out, held, numbers, meta, sems):
    size, (fanout, count) = amps.shape[0], targets.shape
    part = size // XS
    pieces = [pl.ds(i * part, part) for i in range(XS)]
    reads = [
        pltpu.make_async_copy(amps.at[piece], held.at[piece], sems.at[XS, i])
        for i, piece in enumerate(pieces)
    ]
    reads += [
        pltpu.make_async_copy(ref, numbers.at[i], sems.at[XS + 1, i])
        for i, ref in enumerate((targets, slots))
    ]
    for copy in reads:
        copy.start()
    writes = []
    for i, piece in enumerate(pieces):
        reads[i].wait()
        for x in range(XS):
            writes.append(
                pltpu.make_async_copy(held.at[piece], out.at[x, piece], sems.at[x, i])
            )
            writes[-1].start()
    for copy in reads[XS:]:
        copy.wait()
    rows = jnp.concatenate([numbers[0], numbers[1]], axis=0).astype(jnp.float32)
    rows = jnp.pad(rows, ((0, META - 2 * fanout), (0, out.shape[2] - count)))
    meta[...] = rows.astype(meta.dtype)
    for x in range(XS):
        writes.append(
            pltpu.make_async_copy(meta, out.at[x, pl.ds(size, META)], sems.at[x, XS])
        )
        writes[-1].start()
    for copy in writes:
        copy.wait()


def add_products(first, listed, counts, amps, held, total):
    rows = total.shape[1]
    own = (amps.shape[1] - META) // rows
    tiles = [(ref, k) for ref in held for k in range(ref.shape[0])]

    def pair(place, q):
        codes = [listed[place * 8 + 2 * q + i] for i in range(2)]
        parts = []
        for code in codes:
            index = code >> 6
            start = pl.multiple_of((index % own) * rows, rows)
            parts.append(amps[index // own, pl.ds(start, rows), :])
        ref, k = tiles[place - first]
        tasks = jnp.concatenate(parts, axis=0)
        return codes, jnp.dot(tasks, ref[k], preferred_element_type=jnp.float32)

    def add(codes, product):
        for i, code in enumerate(codes):
            total[code & 63] += product[i * rows : (i + 1) * rows]

    for low in range(first, first + len(tiles), 4):
        for codes, product in [pair(place, 0) for place in range(low, low + 4)]:
            add(codes, product)
    for place in range(first, first + len(tiles)):

        def more(q, carry, place=place):
            add(*pair(place, q))
            return carry

        lax.fori_loop(1, (counts[place] + 1) // 2, more, 0)


def early(listed, counts, amps, *refs):
    held, total = refs[:-1], refs[-1]
    total[...] = jnp.zeros_like(total)
    add_products(0, listed, counts, amps, held, total)


def late(first, listed, counts, amps, before, held, out, total):
    total[...] = before[...]
    add_products(first, listed, counts, amps, (held,), total)
    out[...] = total[: out.shape[0]].astype(out.dtype)


def per_device(amplitudes, integrals, executors, residual_slots):
    own, rows, columns = amplitudes.shape[1:]
    fanout = executors.shape[2]
    tasks = own * fanout
    depth = lax.axis_size("tile") // XS
    me = lax.axis_index("tile")
    my_x, my_z = me % XS, me // XS

    vmem = pl.BlockSpec(memory_space=pltpu.VMEM)
    smem = pl.BlockSpec(memory_space=pltpu.SMEM)
    anywhere = pl.BlockSpec(memory_space=pl.ANY)
    flat = own * rows
    packed = pl.pallas_call(
        pack,
        out_shape=jax.ShapeDtypeStruct((XS, flat + META, columns), jnp.bfloat16),
        in_specs=[anywhere] * 3,
        out_specs=anywhere,
        scratch_shapes=[
            pltpu.VMEM((flat, columns), jnp.bfloat16),
            pltpu.VMEM((2, fanout, own), jnp.int32),
            pltpu.VMEM((META, columns), jnp.bfloat16),
            pltpu.SemaphoreType.DMA((XS + 2, XS + 1)),
        ],
    )(amplitudes.reshape(flat, columns), executors[0].T, residual_slots[0].T)
    integrals, packed = lax.optimization_barrier((integrals, packed))
    amps = along_x(packed)
    mine = every_fourth(integrals[0])
    mine, amps = lax.optimization_barrier((mine, amps))
    one, near, other = moved(mine, 1, True), moved(mine, 0, True), moved(mine, -1, True)
    far = moved(one, -1)

    numbers = amps[:, flat : flat + 2 * fanout, :own].astype(jnp.int32)
    target = numbers[:, :fanout].reshape(XS * tasks)
    slot = numbers[:, fanout:].reshape(XS * tasks)
    task = jnp.arange(XS * tasks, dtype=jnp.int32)
    source = task // tasks
    code = (source * own + task % own) * 64 + source * RT + slot
    place = jnp.arange(depth, dtype=jnp.int32)
    toward = 1 - 2 * (lax.axis_index("irrep") % 2)
    apart = toward * jnp.array(APART, jnp.int32)
    place_z = (my_z + apart) % SKIP + SKIP * (place % SKIP)
    hot = target[None, :] == (place_z * XS + my_x)[:, None]
    hot_bf16 = hot.astype(jnp.bfloat16)
    earlier = (task[:, None] < task[None, :]).astype(jnp.bfloat16)
    rank = jnp.dot(hot_bf16, earlier, preferred_element_type=jnp.float32).astype(jnp.int32)
    counts = jnp.sum(hot.astype(jnp.int32), axis=1)
    ranks = jnp.arange(8, dtype=jnp.int32)
    chosen = hot[:, None, :] & (rank[:, None, :] == ranks[None, :, None])
    spare = XS * RT
    listed = spare + jnp.sum(jnp.where(chosen, code - spare, 0), axis=2)
    listed = listed.reshape(depth * 8)

    total_shape = (spare + 1, rows, columns)
    params = pltpu.CompilerParams(vmem_limit_bytes=12 * 1024 * 1024)
    total = pl.pallas_call(
        early,
        out_shape=jax.ShapeDtypeStruct(total_shape, jnp.float32),
        in_specs=[smem] * 2 + [vmem] * 4,
        out_specs=vmem,
        compiler_params=params,
        cost_estimate=pl.CostEstimate(flops=1 << 28, bytes_accessed=1 << 23, transcendentals=0),
    )(listed, counts, amps, near, one, other)
    partial = pl.pallas_call(
        functools.partial(late, 12),
        out_shape=jax.ShapeDtypeStruct((spare, rows, columns), jnp.bfloat16),
        in_specs=[smem] * 2 + [vmem] * 3,
        out_specs=vmem,
        scratch_shapes=[pltpu.VMEM(total_shape, jnp.float32)],
        compiler_params=params,
        cost_estimate=pl.CostEstimate(flops=1 << 28, bytes_accessed=1 << 23, transcendentals=0),
    )(listed, counts, amps, total, far)
    back = along_x(partial).reshape(XS, RT, rows, columns)
    return jnp.sum(back.astype(jnp.float32), axis=0).astype(jnp.bfloat16)[None]


def solution(mesh):
    placed = (
        P("irrep", "tile", None, None),
        P("irrep", "tile", None, None),
        P("irrep", "tile", None),
        P("irrep", "tile", None),
    )
    return jax.shard_map(
        per_device,
        mesh=mesh,
        in_specs=placed,
        out_specs=P("irrep", "tile", None, None),
        check_vma=False,
    )
```

```python
import functools
import jax
import jax.numpy as jnp
from jax import lax
from jax.experimental import pallas as pl
from jax.experimental.pallas import tpu as pltpu
from jax.sharding import PartitionSpec as P

RT = 8
XS = 4
SKIP = 4

META = 16

APART = (0,) * 4 + (1,) * 4 + (-1,) * 4 + (2,) * 4


def moved(block, dz, flip=False):
    groups, tiles = lax.axis_size("irrep"), lax.axis_size("tile")
    route = []
    for g in range(groups):
        for t in range(tiles):
            to = (t + (dz if g % 2 else -dz) * XS) % tiles
            route.append((g * tiles + t, (g ^ 1 if flip else g) * tiles + to))
    return lax.ppermute(block, ("irrep", "tile"), route)


def along_x(block):
    tiles = lax.axis_size("tile")
    rows = [list(range(low, low + XS)) for low in range(0, tiles, XS)]
    return lax.all_to_all(
        block, "tile", split_axis=0, concat_axis=0, axis_index_groups=rows, tiled=True
    )


def every_fourth(block):
    tiles = lax.axis_size("tile")
    step = SKIP * XS
    groups = [list(range(low, tiles, step)) for low in range(step)]
    return lax.all_gather(block, "tile", axis=0, axis_index_groups=groups, tiled=True)


def pack(amps, targets, slots, out, held, numbers, meta, sems):
    size, (fanout, count) = amps.shape[0], targets.shape
    part = size // XS
    pieces = [pl.ds(i * part, part) for i in range(XS)]
    reads = [
        pltpu.make_async_copy(amps.at[piece], held.at[piece], sems.at[XS, i])
        for i, piece in enumerate(pieces)
    ]
    reads += [
        pltpu.make_async_copy(ref, numbers.at[i], sems.at[XS + 1, i])
        for i, ref in enumerate((targets, slots))
    ]
    for copy in reads:
        copy.start()
    writes = []
    for i, piece in enumerate(pieces):
        reads[i].wait()
        for x in range(XS):
            writes.append(
                pltpu.make_async_copy(held.at[piece], out.at[x, piece], sems.at[x, i])
            )
            writes[-1].start()
    for copy in reads[XS:]:
        copy.wait()
    rows = jnp.concatenate([numbers[0], numbers[1]], axis=0).astype(jnp.float32)
    rows = jnp.pad(rows, ((0, META - 2 * fanout), (0, out.shape[2] - count)))
    meta[...] = rows.astype(meta.dtype)
    for x in range(XS):
        writes.append(
            pltpu.make_async_copy(meta, out.at[x, pl.ds(size, META)], sems.at[x, XS])
        )
        writes[-1].start()
    for copy in writes:
        copy.wait()


def add_products(first, listed, counts, amps, held, total):
    rows = total.shape[1]
    own = (amps.shape[1] - META) // rows
    tiles = [(ref, k) for ref in held for k in range(ref.shape[0])]

    def pair(place, q):
        codes = [listed[place * 8 + 2 * q + i] for i in range(2)]
        parts = []
        for code in codes:
            index = code >> 6
            start = pl.multiple_of((index % own) * rows, rows)
            parts.append(amps[index // own, pl.ds(start, rows), :])
        ref, k = tiles[place - first]
        tasks = jnp.concatenate(parts, axis=0)
        return codes, jnp.dot(tasks, ref[k], preferred_element_type=jnp.float32)

    def add(codes, product):
        for i, code in enumerate(codes):
            total[code & 63] += product[i * rows : (i + 1) * rows]

    for low in range(first, first + len(tiles), 4):
        for codes, product in [pair(place, 0) for place in range(low, low + 4)]:
            add(codes, product)
    for place in range(first, first + len(tiles)):

        def more(q, carry, place=place):
            add(*pair(place, q))
            return carry

        lax.fori_loop(1, (counts[place] + 1) // 2, more, 0)


def early(listed, counts, amps, *refs):
    held, total = refs[:-1], refs[-1]
    total[...] = jnp.zeros_like(total)
    add_products(0, listed, counts, amps, held, total)


def late(first, listed, counts, amps, before, held, out, total):
    total[...] = before[...]
    add_products(first, listed, counts, amps, (held,), total)
    out[...] = total[: out.shape[0]].astype(out.dtype)


def per_device(amplitudes, integrals, executors, residual_slots):
    own, rows, columns = amplitudes.shape[1:]
    fanout = executors.shape[2]
    tasks = own * fanout
    depth = lax.axis_size("tile") // XS
    me = lax.axis_index("tile")
    my_x, my_z = me % XS, me // XS

    vmem = pl.BlockSpec(memory_space=pltpu.VMEM)
    smem = pl.BlockSpec(memory_space=pltpu.SMEM)
    anywhere = pl.BlockSpec(memory_space=pl.ANY)
    flat = own * rows
    packed = pl.pallas_call(
        pack,
        out_shape=jax.ShapeDtypeStruct((XS, flat + META, columns), jnp.bfloat16),
        in_specs=[anywhere] * 3,
        out_specs=anywhere,
        scratch_shapes=[
            pltpu.VMEM((flat, columns), jnp.bfloat16),
            pltpu.VMEM((2, fanout, own), jnp.int32),
            pltpu.VMEM((META, columns), jnp.bfloat16),
            pltpu.SemaphoreType.DMA((XS + 2, XS + 1)),
        ],
    )(amplitudes.reshape(flat, columns), executors[0].T, residual_slots[0].T)
    integrals, packed = lax.optimization_barrier((integrals, packed))
    amps = along_x(packed)
    mine = every_fourth(integrals[0])
    mine, amps = lax.optimization_barrier((mine, amps))
    one, near, other = moved(mine, 1, True), moved(mine, 0, True), moved(mine, -1, True)
    far = moved(one, -1)

    numbers = amps[:, flat : flat + 2 * fanout, :own].astype(jnp.int32)
    target = numbers[:, :fanout].reshape(XS * tasks)
    slot = numbers[:, fanout:].reshape(XS * tasks)
    task = jnp.arange(XS * tasks, dtype=jnp.int32)
    source = task // tasks
    code = (source * own + task % own) * 64 + source * RT + slot
    place = jnp.arange(depth, dtype=jnp.int32)
    toward = 2 * (lax.axis_index("irrep") % 2) - 1
    apart = toward * jnp.array(APART, jnp.int32)
    place_z = (my_z + apart) % SKIP + SKIP * (place % SKIP)
    hot = target[None, :] == (place_z * XS + my_x)[:, None]
    hot_bf16 = hot.astype(jnp.bfloat16)
    earlier = (task[:, None] < task[None, :]).astype(jnp.bfloat16)
    rank = jnp.dot(hot_bf16, earlier, preferred_element_type=jnp.float32).astype(jnp.int32)
    counts = jnp.sum(hot.astype(jnp.int32), axis=1)
    ranks = jnp.arange(8, dtype=jnp.int32)
    chosen = hot[:, None, :] & (rank[:, None, :] == ranks[None, :, None])
    spare = XS * RT
    listed = spare + jnp.sum(jnp.where(chosen, code - spare, 0), axis=2)
    listed = listed.reshape(depth * 8)

    total_shape = (spare + 1, rows, columns)
    params = pltpu.CompilerParams(vmem_limit_bytes=12 * 1024 * 1024)
    total = pl.pallas_call(
        early,
        out_shape=jax.ShapeDtypeStruct(total_shape, jnp.float32),
        in_specs=[smem] * 2 + [vmem] * 4,
        out_specs=vmem,
        compiler_params=params,
        cost_estimate=pl.CostEstimate(flops=1 << 28, bytes_accessed=1 << 23, transcendentals=0),
    )(listed, counts, amps, near, one, other)
    partial = pl.pallas_call(
        functools.partial(late, 12),
        out_shape=jax.ShapeDtypeStruct((spare, rows, columns), jnp.bfloat16),
        in_specs=[smem] * 2 + [vmem] * 3,
        out_specs=vmem,
        scratch_shapes=[pltpu.VMEM(total_shape, jnp.float32)],
        compiler_params=params,
        cost_estimate=pl.CostEstimate(flops=1 << 28, bytes_accessed=1 << 23, transcendentals=0),
    )(listed, counts, amps, total, far)
    back = along_x(partial).reshape(XS, RT, rows, columns)
    return jnp.sum(back.astype(jnp.float32), axis=0).astype(jnp.bfloat16)[None]


def solution(mesh):
    placed = (
        P("irrep", "tile", None, None),
        P("irrep", "tile", None, None),
        P("irrep", "tile", None),
        P("irrep", "tile", None),
    )
    return jax.shard_map(
        per_device,
        mesh=mesh,
        in_specs=placed,
        out_specs=P("irrep", "tile", None, None),
        check_vma=False,
    )
```

```python
import functools
import jax
import jax.numpy as jnp
from jax import lax
from jax.experimental import pallas as pl
from jax.experimental.pallas import tpu as pltpu
from jax.sharding import PartitionSpec as P

RT = 8
XS = 4
SKIP = 4

META = 16

APART = (0,) * 4 + (1,) * 4 + (-1,) * 4 + (2,) * 4


def moved(block, dz, flip=False):
    groups, tiles = lax.axis_size("irrep"), lax.axis_size("tile")
    route = []
    for g in range(groups):
        for t in range(tiles):
            to = (t + (dz if g % 2 else -dz) * XS) % tiles
            route.append((g * tiles + t, (g ^ 1 if flip else g) * tiles + to))
    return lax.ppermute(block, ("irrep", "tile"), route)


def along_x(block):
    tiles = lax.axis_size("tile")
    rows = [list(range(low, low + XS)) for low in range(0, tiles, XS)]
    return lax.all_to_all(
        block, "tile", split_axis=0, concat_axis=0, axis_index_groups=rows, tiled=True
    )


def every_fourth(block):
    tiles = lax.axis_size("tile")
    step = SKIP * XS
    groups = [list(range(low, tiles, step)) for low in range(step)]
    return lax.all_gather(block, "tile", axis=0, axis_index_groups=groups, tiled=True)


def pack(amps, targets, slots, out, held, numbers, meta, sems):
    size, (fanout, count) = amps.shape[0], targets.shape
    part = size // XS
    pieces = [pl.ds(i * part, part) for i in range(XS)]
    reads = [
        pltpu.make_async_copy(amps.at[piece], held.at[piece], sems.at[XS, i])
        for i, piece in enumerate(pieces)
    ]
    reads += [
        pltpu.make_async_copy(ref, numbers.at[i], sems.at[XS + 1, i])
        for i, ref in enumerate((targets, slots))
    ]
    for copy in reads:
        copy.start()
    writes = []
    for i, piece in enumerate(pieces):
        reads[i].wait()
        for x in range(XS):
            writes.append(
                pltpu.make_async_copy(held.at[piece], out.at[x, piece], sems.at[x, i])
            )
            writes[-1].start()
    for copy in reads[XS:]:
        copy.wait()
    rows = jnp.concatenate([numbers[0], numbers[1]], axis=0).astype(jnp.float32)
    rows = jnp.pad(rows, ((0, META - 2 * fanout), (0, out.shape[2] - count)))
    meta[...] = rows.astype(meta.dtype)
    for x in range(XS):
        writes.append(
            pltpu.make_async_copy(meta, out.at[x, pl.ds(size, META)], sems.at[x, XS])
        )
        writes[-1].start()
    for copy in writes:
        copy.wait()


def add_products(first, listed, counts, amps, held, total):
    rows = total.shape[1]
    own = (amps.shape[1] - META) // rows
    tiles = [(ref, k) for ref in held for k in range(ref.shape[0])]

    def pair(place, q):
        codes = [listed[place * 8 + 2 * q + i] for i in range(2)]
        parts = []
        for code in codes:
            index = code >> 6
            start = pl.multiple_of((index % own) * rows, rows)
            parts.append(amps[index // own, pl.ds(start, rows), :])
        ref, k = tiles[place - first]
        tasks = jnp.concatenate(parts, axis=0)
        return codes, jnp.dot(tasks, ref[k], preferred_element_type=jnp.float32)

    def add(codes, product):
        for i, code in enumerate(codes):
            total[code & 63] += product[i * rows : (i + 1) * rows]

    for low in range(first, first + len(tiles), 4):
        for codes, product in [pair(place, 0) for place in range(low, low + 4)]:
            add(codes, product)
    for place in range(first, first + len(tiles)):

        def more(q, carry, place=place):
            add(*pair(place, q))
            return carry

        lax.fori_loop(1, (counts[place] + 1) // 2, more, 0)


def early(listed, counts, amps, *refs):
    held, total = refs[:-1], refs[-1]
    total[...] = jnp.zeros_like(total)
    add_products(0, listed, counts, amps, held, total)


def late(first, listed, counts, amps, before, held, out, total):
    total[...] = before[...]
    add_products(first, listed, counts, amps, (held,), total)
    out[...] = total[: out.shape[0]].astype(out.dtype)


def per_device(amplitudes, integrals, executors, residual_slots):
    own, rows, columns = amplitudes.shape[1:]
    fanout = executors.shape[2]
    tasks = own * fanout
    depth = lax.axis_size("tile") // XS
    me = lax.axis_index("tile")
    my_x, my_z = me % XS, me // XS

    vmem = pl.BlockSpec(memory_space=pltpu.VMEM)
    smem = pl.BlockSpec(memory_space=pltpu.SMEM)
    anywhere = pl.BlockSpec(memory_space=pl.ANY)
    flat = own * rows
    packed = pl.pallas_call(
        pack,
        out_shape=jax.ShapeDtypeStruct((XS, flat + META, columns), jnp.bfloat16),
        in_specs=[anywhere] * 3,
        out_specs=anywhere,
        scratch_shapes=[
            pltpu.VMEM((flat, columns), jnp.bfloat16),
            pltpu.VMEM((2, fanout, own), jnp.int32),
            pltpu.VMEM((META, columns), jnp.bfloat16),
            pltpu.SemaphoreType.DMA((XS + 2, XS + 1)),
        ],
    )(amplitudes.reshape(flat, columns), executors[0].T, residual_slots[0].T)
    integrals, packed = lax.optimization_barrier((integrals, packed))
    amps = along_x(packed)
    mine = every_fourth(integrals[0])
    one, near, other = moved(mine, 1, True), moved(mine, 0, True), moved(mine, -1, True)
    one, amps = lax.optimization_barrier((one, amps))
    far = moved(one, -1)

    numbers = amps[:, flat : flat + 2 * fanout, :own].astype(jnp.int32)
    target = numbers[:, :fanout].reshape(XS * tasks)
    slot = numbers[:, fanout:].reshape(XS * tasks)
    task = jnp.arange(XS * tasks, dtype=jnp.int32)
    source = task // tasks
    code = (source * own + task % own) * 64 + source * RT + slot
    place = jnp.arange(depth, dtype=jnp.int32)
    toward = 2 * (lax.axis_index("irrep") % 2) - 1
    apart = toward * jnp.array(APART, jnp.int32)
    place_z = (my_z + apart) % SKIP + SKIP * (place % SKIP)
    hot = target[None, :] == (place_z * XS + my_x)[:, None]
    hot_bf16 = hot.astype(jnp.bfloat16)
    earlier = (task[:, None] < task[None, :]).astype(jnp.bfloat16)
    rank = jnp.dot(hot_bf16, earlier, preferred_element_type=jnp.float32).astype(jnp.int32)
    counts = jnp.sum(hot.astype(jnp.int32), axis=1)
    ranks = jnp.arange(8, dtype=jnp.int32)
    chosen = hot[:, None, :] & (rank[:, None, :] == ranks[None, :, None])
    spare = XS * RT
    listed = spare + jnp.sum(jnp.where(chosen, code - spare, 0), axis=2)
    listed = listed.reshape(depth * 8)

    total_shape = (spare + 1, rows, columns)
    params = pltpu.CompilerParams(vmem_limit_bytes=12 * 1024 * 1024)
    total = pl.pallas_call(
        early,
        out_shape=jax.ShapeDtypeStruct(total_shape, jnp.float32),
        in_specs=[smem] * 2 + [vmem] * 4,
        out_specs=vmem,
        compiler_params=params,
        cost_estimate=pl.CostEstimate(flops=1 << 28, bytes_accessed=1 << 23, transcendentals=0),
    )(listed, counts, amps, near, one, other)
    partial = pl.pallas_call(
        functools.partial(late, 12),
        out_shape=jax.ShapeDtypeStruct((spare, rows, columns), jnp.bfloat16),
        in_specs=[smem] * 2 + [vmem] * 3,
        out_specs=vmem,
        scratch_shapes=[pltpu.VMEM(total_shape, jnp.float32)],
        compiler_params=params,
        cost_estimate=pl.CostEstimate(flops=1 << 28, bytes_accessed=1 << 23, transcendentals=0),
    )(listed, counts, amps, total, far)
    back = along_x(partial).reshape(XS, RT, rows, columns)
    return jnp.sum(back.astype(jnp.float32), axis=0).astype(jnp.bfloat16)[None]


def solution(mesh):
    placed = (
        P("irrep", "tile", None, None),
        P("irrep", "tile", None, None),
        P("irrep", "tile", None),
        P("irrep", "tile", None),
    )
    return jax.shard_map(
        per_device,
        mesh=mesh,
        in_specs=placed,
        out_specs=P("irrep", "tile", None, None),
        check_vma=False,
    )
```

```python
import functools
import jax
import jax.numpy as jnp
from jax import lax
from jax.experimental import pallas as pl
from jax.experimental.pallas import tpu as pltpu
from jax.sharding import PartitionSpec as P

RT = 8
XS = 4
SKIP = 4

META = 16

APART = (0,) * 4 + (1,) * 4 + (-1,) * 4 + (2,) * 4


def moved(block, dz, flip=False):
    groups, tiles = lax.axis_size("irrep"), lax.axis_size("tile")
    route = []
    for g in range(groups):
        for t in range(tiles):
            to = (t + (dz if g % 2 else -dz) * XS) % tiles
            route.append((g * tiles + t, (g ^ 1 if flip else g) * tiles + to))
    return lax.ppermute(block, ("irrep", "tile"), route)


def along_x(block):
    tiles = lax.axis_size("tile")
    rows = [list(range(low, low + XS)) for low in range(0, tiles, XS)]
    return lax.all_to_all(
        block, "tile", split_axis=0, concat_axis=0, axis_index_groups=rows, tiled=True
    )


def every_fourth(block):
    tiles = lax.axis_size("tile")
    step = SKIP * XS
    groups = [list(range(low, tiles, step)) for low in range(step)]
    return lax.all_gather(block, "tile", axis=0, axis_index_groups=groups, tiled=True)


def pack(amps, targets, slots, out, held, numbers, meta, sems):
    size, (fanout, count) = amps.shape[0], targets.shape
    part = size // XS
    pieces = [pl.ds(i * part, part) for i in range(XS)]
    reads = [
        pltpu.make_async_copy(amps.at[piece], held.at[piece], sems.at[XS, i])
        for i, piece in enumerate(pieces)
    ]
    reads += [
        pltpu.make_async_copy(ref, numbers.at[i], sems.at[XS + 1, i])
        for i, ref in enumerate((targets, slots))
    ]
    for copy in reads:
        copy.start()
    writes = []
    for i, piece in enumerate(pieces):
        reads[i].wait()
        for x in range(XS):
            writes.append(
                pltpu.make_async_copy(held.at[piece], out.at[x, piece], sems.at[x, i])
            )
            writes[-1].start()
    for copy in reads[XS:]:
        copy.wait()
    rows = jnp.concatenate([numbers[0], numbers[1]], axis=0).astype(jnp.float32)
    rows = jnp.pad(rows, ((0, META - 2 * fanout), (0, out.shape[2] - count)))
    meta[...] = rows.astype(meta.dtype)
    for x in range(XS):
        writes.append(
            pltpu.make_async_copy(meta, out.at[x, pl.ds(size, META)], sems.at[x, XS])
        )
        writes[-1].start()
    for copy in writes:
        copy.wait()


def add_products(first, listed, counts, amps, held, total, before=None):
    rows = total.shape[1]
    own = (amps.shape[1] - META) // rows
    tiles = [(ref, k) for ref in held for k in range(ref.shape[0])]

    def pair(place, q):
        codes = [listed[place * 8 + 2 * q + i] for i in range(2)]
        parts = []
        for code in codes:
            index = code >> 6
            start = pl.multiple_of((index % own) * rows, rows)
            parts.append(amps[index // own, pl.ds(start, rows), :])
        ref, k = tiles[place - first]
        tasks = jnp.concatenate(parts, axis=0)
        return codes, jnp.dot(tasks, ref[k], preferred_element_type=jnp.float32)

    def add(codes, product):
        for i, code in enumerate(codes):
            total[code & 63] += product[i * rows : (i + 1) * rows]

    for low in range(first, first + len(tiles), 4):
        products = [pair(place, 0) for place in range(low, low + 4)]
        if before is not None and low == first:
            total[...] = before[...]
        for codes, product in products:
            add(codes, product)
    for place in range(first, first + len(tiles)):

        def more(q, carry, place=place):
            add(*pair(place, q))
            return carry

        lax.fori_loop(1, (counts[place] + 1) // 2, more, 0)


def early(listed, counts, amps, *refs):
    held, total = refs[:-1], refs[-1]
    total[...] = jnp.zeros_like(total)
    add_products(0, listed, counts, amps, held, total)


def late(first, listed, counts, amps, before, held, out, total):
    add_products(first, listed, counts, amps, (held,), total, before)
    out[...] = total[: out.shape[0]].astype(out.dtype)


def per_device(amplitudes, integrals, executors, residual_slots):
    own, rows, columns = amplitudes.shape[1:]
    fanout = executors.shape[2]
    tasks = own * fanout
    depth = lax.axis_size("tile") // XS
    me = lax.axis_index("tile")
    my_x, my_z = me % XS, me // XS

    vmem = pl.BlockSpec(memory_space=pltpu.VMEM)
    smem = pl.BlockSpec(memory_space=pltpu.SMEM)
    anywhere = pl.BlockSpec(memory_space=pl.ANY)
    flat = own * rows
    packed = pl.pallas_call(
        pack,
        out_shape=jax.ShapeDtypeStruct((XS, flat + META, columns), jnp.bfloat16),
        in_specs=[anywhere] * 3,
        out_specs=anywhere,
        scratch_shapes=[
            pltpu.VMEM((flat, columns), jnp.bfloat16),
            pltpu.VMEM((2, fanout, own), jnp.int32),
            pltpu.VMEM((META, columns), jnp.bfloat16),
            pltpu.SemaphoreType.DMA((XS + 2, XS + 1)),
        ],
    )(amplitudes.reshape(flat, columns), executors[0].T, residual_slots[0].T)
    integrals, packed = lax.optimization_barrier((integrals, packed))
    amps = along_x(packed)
    mine = every_fourth(integrals[0])
    one, near, other = moved(mine, 1, True), moved(mine, 0, True), moved(mine, -1, True)
    one, amps = lax.optimization_barrier((one, amps))
    far = moved(one, -1)

    numbers = amps[:, flat : flat + 2 * fanout, :own].astype(jnp.int32)
    target = numbers[:, :fanout].reshape(XS * tasks)
    slot = numbers[:, fanout:].reshape(XS * tasks)
    task = jnp.arange(XS * tasks, dtype=jnp.int32)
    source = task // tasks
    code = (source * own + task % own) * 64 + source * RT + slot
    place = jnp.arange(depth, dtype=jnp.int32)
    toward = 2 * (lax.axis_index("irrep") % 2) - 1
    apart = toward * jnp.array(APART, jnp.int32)
    place_z = (my_z + apart) % SKIP + SKIP * (place % SKIP)
    hot = target[None, :] == (place_z * XS + my_x)[:, None]
    hot_bf16 = hot.astype(jnp.bfloat16)
    earlier = (task[:, None] < task[None, :]).astype(jnp.bfloat16)
    rank = jnp.dot(hot_bf16, earlier, preferred_element_type=jnp.float32).astype(jnp.int32)
    counts = jnp.sum(hot.astype(jnp.int32), axis=1)
    ranks = jnp.arange(8, dtype=jnp.int32)
    chosen = hot[:, None, :] & (rank[:, None, :] == ranks[None, :, None])
    spare = XS * RT
    listed = spare + jnp.sum(jnp.where(chosen, code - spare, 0), axis=2)
    listed = listed.reshape(depth * 8)

    total_shape = (spare + 1, rows, columns)
    params = pltpu.CompilerParams(vmem_limit_bytes=12 * 1024 * 1024)
    total = pl.pallas_call(
        early,
        out_shape=jax.ShapeDtypeStruct(total_shape, jnp.float32),
        in_specs=[smem] * 2 + [vmem] * 4,
        out_specs=vmem,
        compiler_params=params,
        cost_estimate=pl.CostEstimate(flops=1 << 28, bytes_accessed=1 << 23, transcendentals=0),
    )(listed, counts, amps, near, one, other)
    partial = pl.pallas_call(
        functools.partial(late, 12),
        out_shape=jax.ShapeDtypeStruct((spare, rows, columns), jnp.bfloat16),
        in_specs=[smem] * 2 + [vmem] * 3,
        out_specs=vmem,
        scratch_shapes=[pltpu.VMEM(total_shape, jnp.float32)],
        compiler_params=params,
        cost_estimate=pl.CostEstimate(flops=1 << 28, bytes_accessed=1 << 23, transcendentals=0),
    )(listed, counts, amps, total, far)
    back = along_x(partial).reshape(XS, RT, rows, columns)
    return jnp.sum(back.astype(jnp.float32), axis=0).astype(jnp.bfloat16)[None]


def solution(mesh):
    placed = (
        P("irrep", "tile", None, None),
        P("irrep", "tile", None, None),
        P("irrep", "tile", None),
        P("irrep", "tile", None),
    )
    return jax.shard_map(
        per_device,
        mesh=mesh,
        in_specs=placed,
        out_specs=P("irrep", "tile", None, None),
        check_vma=False,
    )
```
